32 devices in a mesh: grp: 2 (over x), blk: 16 (over z, y, core).
Axes of the slice: x: 2, y: 2, z: 4, core: 2. Of those that a mesh axis runs over, the one named last changes fastest.
Arguments:
- acts: bfloat16 [8192, 5120], P(('grp', 'blk')), parts along dimension 0, may hold values from -6 to 6
- grads: bfloat16 [8192, 20480], P(('grp', 'blk')), parts along dimension 0, may hold values from -6 to 6
- basis_act: bfloat16 [32, 5120], P('blk'), may hold values from -0.078125 to 0.078125
- basis_grad: bfloat16 [64, 20480], P('blk'), may hold values from -0.0390625 to 0.0390625
- eigvals: float32 [64, 32], P('blk'), may hold values from 0.01 to 10
- queries: bfloat16 [32, 64, 32], P('grp', 'blk'), parts along dimension 0, may hold values from -0.29882812 to 0.29882812
- owner: int32 [16], replicated, may hold values from 0 to 15, each once
- seq_of_shard: int32 [32], P('grp'), parts along dimension 0, may hold values from 0 to 1, as said below
Outputs:
- scores: float32 [32, 2], P('grp'), parts along dimension 0
The draws below stay inside these ranges and needn't reach their ends.
There are 2 independent parts, one for each index of `grp`. The reference program is written for one: setup_inputs(seed, part) draws one part's arguments, and reference() takes and returns one part's arrays. A program takes and returns all parts, laid end to end along the dimension named above; an argument that names none is the same for every part. Nothing has to cross between parts.
Inputs may be any that keep to these rules, and one draw needn't show every extreme that they name: `seq_of_shard`: each sequence number is named by exactly 8 entries.
All inputs are finite; a program needn't handle non-finite values.
Results may differ from the reference program's by a relative error of at most 0.006.
Values may be sent and summed in bfloat16 or wider, within the bound.
A program may use at most 128 MiB of HBM per device.

```python
import math
import jax
import jax.numpy as jnp
from jax import lax

D = 5120
FF = 20480
LEN = 2048
TOK_DEV = 256
EA_DEV = 2
ES_DEV = 4
NQ = 16
EA = 32
ES = 64
TOKENS = 4096
N_BLK = 16


def draw_seq_of_shard(key, part):
    key = jax.random.fold_in(key, 7)
    base = jnp.arange(N_BLK, dtype=jnp.int32) // (LEN // TOK_DEV)
    return jax.random.permutation(key, base).astype(jnp.int32)


def block_levels(own_key, dims, cuts, smallest, high):
    factor_of, own = 1.0, jax.random.fold_in(own_key, 6)
    for dim, blocks in cuts:
        steps = jnp.exp(jax.random.uniform(jax.random.fold_in(own, dim), (blocks,), jnp.float32, smallest / len(cuts), high / len(cuts)))
        factor_of = factor_of * jnp.repeat(steps, dims[dim] // blocks).reshape([-1 if axis == dim else 1 for axis in range(len(dims))])
    return factor_of


def gaussian(key, shape, spread, reach, cuts=(), kind=jnp.bfloat16):
    result = spread * jax.random.normal(key, shape, jnp.float32)
    if cuts:
        result = result * block_levels(key, shape, cuts, -0.22, 0.18)
    return jnp.clip(result, -reach, reach).astype(kind)


def setup_inputs(seed: int = 0, part: int = 0) -> dict:
    arg_keys = jax.random.split(jax.random.key(seed), 9)
    own_keys = jax.random.split(jax.random.fold_in(arg_keys[8], part), 9)
    return {
        "acts": gaussian(own_keys[0], (TOKENS, D), 1.0, 6.0, ((0, 16),)),
        "grads": gaussian(own_keys[1], (TOKENS, FF), 1.0, 6.0, ((0, 16),)),
        "basis_act": gaussian(arg_keys[2], (EA, D), D ** -0.5, 0.078125, ((0, 16),)),
        "basis_grad": gaussian(arg_keys[3], (ES, FF), FF ** -0.5, 0.0390625, ((0, 16),)),
        "eigvals": jnp.clip(jnp.exp(math.log(10.0) - 6.9077553 * jax.random.uniform(arg_keys[4], (ES, EA), jnp.float32) ** block_levels(arg_keys[4], (ES, EA), ((0, 16),), -0.2, 0.2)), 0.01, 10.0),
        "queries": gaussian(own_keys[5], (NQ, ES, EA), 0.05, 0.29882812, ((1, 16),)),
        "owner": jax.random.permutation(arg_keys[6], N_BLK).astype(jnp.int32),
        "seq_of_shard": draw_seq_of_shard(jax.random.fold_in(jax.random.fold_in(arg_keys[8], part), 71), part),
    }


damping = 0.1


def reference(acts, grads, basis_act, basis_grad, eigvals, queries, owner, seq_of_shard):
    basis_a = basis_act.reshape(N_BLK, EA_DEV, D)[owner].reshape(EA_DEV * N_BLK, D)
    basis_s = basis_grad.reshape(N_BLK, ES_DEV, FF)[owner].reshape(ES_DEV * N_BLK, FF)
    rot_s = lax.dot_general(grads, basis_s, (((1,), (1,)), ((), ())), preferred_element_type=jnp.float32).astype(jnp.bfloat16)
    rot_a = lax.dot_general(acts, basis_a, (((1,), (1,)), ((), ())), preferred_element_type=jnp.float32).astype(jnp.bfloat16)
    rows_s = rot_s.astype(jnp.float32).reshape(N_BLK, TOK_DEV, ES_DEV * N_BLK)
    rows_a = rot_a.astype(jnp.float32).reshape(N_BLK, TOK_DEV, EA_DEV * N_BLK)
    partial_grad = jnp.einsum('dti,dtj->dij', rows_s, rows_a, precision=lax.Precision.HIGHEST)
    seq_count = TOK_DEV * N_BLK // LEN
    member = (seq_of_shard[None, :] == jnp.arange(seq_count, dtype=jnp.int32)[:, None]).astype(jnp.float32)
    rotated = jnp.einsum('ed,dij->eij', member, partial_grad, precision=lax.Precision.HIGHEST)
    scaled = rotated / LEN / (eigvals + damping)[None]
    return jnp.einsum('qij,eij->qe', queries.astype(jnp.float32), scaled, precision=lax.Precision.HIGHEST)
```

```python
import functools

import jax
import jax.numpy as jnp
from jax import lax
from jax.experimental import pallas as pl
from jax.experimental.pallas import tpu as pltpu
from jax.sharding import PartitionSpec as P

LEN = 2048


damping = 0.1

NZ, NY, NC = 4, 2, 2
ROWS = 16
LANES = 128
MESH = pl.DeviceIdType.MESH


def slot_of(index):
    return (index % NC) * (NY * NZ) + ((index // NC) % NY) * NZ + index // (NC * NY)


def kernel(
    cuts, fold_s, fold_a, width_s, width_a, nq, seqs,
    owner_ref, seq_ref, slab_ref, acts_ref, grads_ref, out_ref,
    buf, acts_v, grads_v, acc_s, rot_a, w_perm, fin,
    load_sem, own_sem, z_send, z_recv, y_send, y_recv, x_send, x_recv, c_send, c_recv, f_send, f_recv,
):
    mine, theirs, shared = cuts
    grp = lax.axis_index("grp")
    me = lax.axis_index("blk")
    core, y, z = me % NC, (me // NC) % NY, me // (NC * NY)
    blocks = NZ * NY * NC
    line = NZ * ROWS
    half = NY * line
    own_row = pl.multiple_of(slot_of(me) * ROWS, ROWS)
    own_line = pl.multiple_of((core * NY + y) * line, line)
    far_line = pl.multiple_of((core * NY + 1 - y) * line, line)
    own_half = pl.multiple_of(core * half, half)
    far_half = pl.multiple_of((1 - core) * half, half)

    loads = [
        pltpu.make_async_copy(acts_ref, acts_v, load_sem.at[0])
    ] + [
        pltpu.make_async_copy(
            grads_ref.at[:, pl.ds(g * width_s, width_s)],
            grads_v.at[:, pl.ds(g * width_s, width_s)],
            load_sem.at[1 + g],
        )
        for g in range(fold_s)
    ]
    own = pltpu.make_async_copy(slab_ref, buf.at[pl.ds(own_row, ROWS), :], own_sem)
    own.start()
    for load in loads:
        load.start()

    barrier = pltpu.get_barrier_semaphore()
    for step in range(1, blocks):
        pl.semaphore_signal(
            barrier, inc=1, device_id={"blk": lax.rem(me + step, blocks)}, device_id_type=MESH
        )
    pl.semaphore_signal(barrier, inc=1, device_id={"grp": 1 - grp}, device_id_type=MESH)
    own.wait()
    pl.semaphore_wait(barrier, blocks)

    passed = [(pl.multiple_of((grp * len(mine) + n) * w, LANES), w) for n, w in enumerate(mine)]
    passed += shared
    other = [(pl.multiple_of(((1 - grp) * len(theirs) + n) * w, LANES), w) for n, w in enumerate(theirs)]

    sent = []

    def send(row, rows, column, send_sem, recv_sem, target):
        start, width = column
        part = buf.at[pl.ds(row, rows), pl.ds(start, width)]
        copy = pltpu.make_async_remote_copy(
            src_ref=part, dst_ref=part, send_sem=send_sem, recv_sem=recv_sem,
            device_id=target, device_id_type=MESH,
        )
        copy.start()
        sent.append(copy)

    def arrived(row, rows, column, recv_sem):
        start, width = column
        part = buf.at[pl.ds(row, rows), pl.ds(start, width)]
        pltpu.make_async_copy(part, part, recv_sem).wait()

    def row_from(step):
        return pl.multiple_of(own_line + lax.rem(z + NZ - step, NZ) * ROWS, ROWS)

    to_y = {"blk": (z * NY + 1 - y) * NC + core}
    to_core = {"blk": (z * NY + y) * NC + 1 - core}
    to_x = {"grp": 1 - grp}

    def z_start(c):
        for step in range(1, NZ):
            target = {"blk": (lax.rem(z + step, NZ) * NY + y) * NC + core}
            send(own_row, ROWS, passed[c], z_send.at[c, step - 1], z_recv.at[c, step - 1], target)

    def z_done(c):
        for step in range(1, NZ):
            arrived(row_from(step), ROWS, passed[c], z_recv.at[c, step - 1])
        send(own_line, line, passed[c], y_send.at[c], y_recv.at[c], to_y)
        if c < len(mine):
            for step in range(1, NZ):
                send(row_from(step), ROWS, passed[c], x_send.at[c, step], x_recv.at[c, step], to_x)

    def y_done(c):
        arrived(far_line, line, passed[c], y_recv.at[c])
        if c < len(mine):
            send(far_line, line, passed[c], x_send.at[c, 0], x_recv.at[c, 0], to_x)
        send(own_half, half, passed[c], c_send.at[c], c_recv.at[c], to_core)

    def x_done(c):
        for step in range(1, NZ):
            arrived(row_from(step), ROWS, other[c], x_recv.at[c, step])
        arrived(far_line, line, other[c], x_recv.at[c, 0])
        k = len(passed) + c
        send(own_half, half, other[c], c_send.at[k], c_recv.at[k], to_core)

    first = [True]

    def multiply(column):
        start, width = column
        if first[0]:
            for load in loads:
                load.wait()
            acc_s[...] = jnp.zeros_like(acc_s)
            first[0] = False
        basis = buf[:, pl.ds(start, width)]
        for g in range(fold_s):
            at = pl.multiple_of(g * width_s + start, LANES)
            acc_s[g] += lax.dot_general(
                grads_v[:, pl.ds(at, width)], basis,
                (((1,), (1,)), ((), ())), preferred_element_type=jnp.float32,
            )

    def side():
        tokens, lanes = acts_v.shape[0], blocks * ROWS
        lane = lax.broadcasted_iota(jnp.int32, (tokens, lanes), 1)
        basis = buf[:, pl.ds(width_s, width_a)]
        per = ROWS // fold_a
        total = jnp.zeros((tokens, lanes), jnp.float32)
        for h in range(fold_a):
            part = lax.dot_general(
                acts_v[:, pl.ds(h * width_a, width_a)], basis,
                (((1,), (1,)), ((), ())), preferred_element_type=jnp.float32,
            )
            total += jnp.where((lane % ROWS) // per == h, part, 0.0)
        shift = per
        while shift < ROWS:
            total += pltpu.roll(total, lanes - shift, 1)
            shift *= 2
        row = lax.broadcasted_iota(jnp.int32, (lanes, LANES), 0)
        position = lax.broadcasted_iota(jnp.int32, (lanes, LANES), 1) % (per * blocks)
        place = jnp.zeros((lanes, LANES), jnp.int32)
        for k in range(blocks):
            place = jnp.where(position // per == k, slot_of(owner_ref[k]), place)
        pick = jnp.where(row == place * ROWS + position % per, 1.0, 0.0).astype(jnp.bfloat16)
        rot_a[...] = jnp.dot(
            total.astype(jnp.bfloat16), pick, preferred_element_type=jnp.float32
        ).astype(jnp.bfloat16)
        row = lax.broadcasted_iota(jnp.int32, (lanes, lanes), 0)
        column = lax.broadcasted_iota(jnp.int32, (lanes, lanes), 1)
        place = jnp.zeros((lanes, lanes), jnp.int32)
        for k in range(blocks):
            place = jnp.where(column // ROWS == slot_of(k), slot_of(owner_ref[k]), place)
        move = (row // ROWS == place) & (row % ROWS == column % ROWS)
        w_perm[...] = jnp.dot(
            jnp.where(move, 1.0, 0.0).astype(jnp.bfloat16),
            buf[:, pl.ds(width_s + width_a, LANES)],
            preferred_element_type=jnp.float32,
        )

    def work(k, column):
        arrived(far_half, half, column, c_recv.at[k])
        if isinstance(column[0], int) and column[0] >= width_s:
            side()
        else:
            multiply(column)

    for c in range(len(passed)):
        z_start(c)
    count = len(passed)
    for s in range(count + 4):
        if s < count:
            z_done(s)
        if 0 <= s - 1 < count:
            y_done(s - 1)
        if 0 <= s - 2 < len(other):
            x_done(s - 2)
        if 0 <= s - 3 < len(other):
            work(count + s - 3, other[s - 3])
        if 0 <= s - 2 < count:
            work(s - 2, passed[s - 2])

    tokens, lanes = grads_v.shape[0], blocks * ROWS
    per = ROWS // fold_s
    lane = lax.broadcasted_iota(jnp.int32, (tokens, lanes), 1)
    total = jnp.zeros((tokens, lanes), jnp.float32)
    for g in range(fold_s):
        total += jnp.where((lane % ROWS) // per == g, acc_s[g], 0.0)
    shift = per
    while shift < ROWS:
        total += pltpu.roll(total, lanes - shift, 1)
        shift *= 2
    partial = lax.dot_general(
        total.astype(jnp.bfloat16), rot_a[...],
        (((0,), (0,)), ((), ())), preferred_element_type=jnp.float32,
    )
    row = lax.broadcasted_iota(jnp.int32, (lanes, LANES), 0)
    lane = lax.broadcasted_iota(jnp.int32, (lanes, LANES), 1)
    partial = jnp.where(row % ROWS == lane // (LANES // per), partial, 0.0)
    partial = jnp.sum(partial.reshape(blocks, ROWS, LANES), axis=1, keepdims=True)
    terms = jnp.sum(w_perm[...].reshape(blocks, nq, LANES) * partial, axis=0)
    score = jnp.sum(terms, axis=1, keepdims=True)
    row = lax.broadcasted_iota(jnp.int32, (nq, LANES), 0)
    lane = lax.broadcasted_iota(jnp.int32, (nq, LANES), 1)
    seq = seq_ref[me]
    keep = (lane % nq == row) & (lane // nq == seq)
    fin[me] = jnp.sum(jnp.where(keep, score, 0.0), axis=0, keepdims=True)
    for step in range(1, blocks):
        copy = pltpu.make_async_remote_copy(
            src_ref=fin.at[me], dst_ref=fin.at[me],
            send_sem=f_send.at[step - 1], recv_sem=f_recv.at[step - 1],
            device_id={"blk": lax.rem(me + step, blocks)}, device_id_type=MESH,
        )
        copy.start()
        sent.append(copy)
    for step in range(1, blocks):
        part = fin.at[lax.rem(me + blocks - step, blocks)]
        pltpu.make_async_copy(part, part, f_recv.at[step - 1]).wait()
    final = jnp.sum(fin[...], axis=0)
    outs = []
    for e in range(seqs):
        outs.append(jnp.sum(jnp.where(lane == e * nq + row, final, 0.0), axis=1, keepdims=True))
    column = lax.broadcasted_iota(jnp.int32, (nq, seqs), 1)
    result = jnp.zeros((nq, seqs), jnp.float32)
    for e in range(seqs):
        result = jnp.where(column == e, outs[e], result)
    out_ref[...] = result
    for copy in sent:
        copy.wait_send()


def fused(acts, grads, basis_act, basis_grad, eigvals, queries, owner, seq_of_shard):
    blocks = NZ * NY * NC
    tokens = acts.shape[0]
    nq = queries.shape[0]
    seqs = tokens * blocks // LEN
    fold_a = ROWS // basis_act.shape[0]
    fold_s = ROWS // basis_grad.shape[0]
    width_a = basis_act.shape[1] // fold_a
    width_s = basis_grad.shape[1] // fold_s

    def folded(block, fold, width):
        return jnp.concatenate([block[:, g * width:(g + 1) * width] for g in range(fold)], axis=0)

    weights = queries.astype(jnp.float32) / LEN / (eigvals + damping)[None]
    weights = weights.reshape(nq, LANES).astype(jnp.bfloat16)
    slab = jnp.concatenate(
        [folded(basis_grad, fold_s, width_s), folded(basis_act, fold_a, width_a), weights], axis=1
    )
    total = slab.shape[1]
    unit = width_s // 10
    mine = [unit] * 4
    shared = [
        (width_s, width_a + LANES),
        (8 * unit, unit),
        (9 * unit, unit),
    ]
    passed = len(mine) + len(shared)
    rows = blocks * ROWS
    dma = pltpu.SemaphoreType.DMA
    vmem = pl.BlockSpec(memory_space=pltpu.VMEM)
    smem = pl.BlockSpec(memory_space=pltpu.SMEM)
    anywhere = pl.BlockSpec(memory_space=pl.ANY)
    return pl.pallas_call(
        functools.partial(
            kernel, (mine, mine, shared), fold_s, fold_a, width_s, width_a, nq, seqs
        ),
        out_shape=jax.ShapeDtypeStruct((nq, seqs), jnp.float32),
        in_specs=[smem, smem, anywhere, anywhere, anywhere],
        out_specs=vmem,
        scratch_shapes=[
            pltpu.VMEM((rows, total), jnp.bfloat16),
            pltpu.VMEM(acts.shape, jnp.bfloat16),
            pltpu.VMEM(grads.shape, jnp.bfloat16),
            pltpu.VMEM((fold_s, tokens, rows), jnp.float32),
            pltpu.VMEM((tokens, LANES), jnp.bfloat16),
            pltpu.VMEM((rows, LANES), jnp.float32),
            pltpu.VMEM((blocks, 1, LANES), jnp.float32),
            dma((1 + fold_s,)),
            dma,
            dma((passed, NZ - 1)),
            dma((passed, NZ - 1)),
            dma((passed,)),
            dma((passed,)),
            dma((len(mine), NZ)),
            dma((len(mine), NZ)),
            dma((passed + len(mine),)),
            dma((passed + len(mine),)),
            dma((blocks - 1,)),
            dma((blocks - 1,)),
        ],
        compiler_params=pltpu.CompilerParams(
            collective_id=0, has_side_effects=True, vmem_limit_bytes=48 * 1024 * 1024
        ),
    )(owner, seq_of_shard, slab, acts, grads)


def reorder(rotated_dev, owner, block):
    width = rotated_dev.shape[1]
    column = jnp.arange(width, dtype=jnp.int32)
    source = owner[column // block] * block + column % block
    return jnp.take(rotated_dev, source, axis=1)


def shards(acts, grads, basis_act, basis_grad, eigvals, queries, owner, seq_of_shard):
    blocks = lax.axis_size("blk")
    block_a = basis_act.shape[0]
    block_s = basis_grad.shape[0]
    rot_a_dev = lax.dot_general(
        acts,
        lax.all_gather(basis_act, "blk", axis=0, tiled=True),
        (((1,), (1,)), ((), ())),
        preferred_element_type=jnp.float32,
    )
    rot_s_dev = lax.dot_general(
        grads,
        lax.all_gather(basis_grad, "blk", axis=0, tiled=True),
        (((1,), (1,)), ((), ())),
        preferred_element_type=jnp.float32,
    )
    rot_a = reorder(rot_a_dev, owner, block_a).astype(jnp.bfloat16)
    rot_s = reorder(rot_s_dev, owner, block_s).astype(jnp.bfloat16)
    partial_grad = lax.dot_general(
        rot_s, rot_a, (((0,), (0,)), ((), ())), preferred_element_type=jnp.float32
    )
    seq_count = acts.shape[0] * blocks // LEN
    seq_ids = jnp.arange(seq_count, dtype=jnp.int32)
    received = lax.all_to_all(
        partial_grad[None].astype(jnp.bfloat16), "blk", split_axis=1, concat_axis=0, tiled=True
    ).astype(jnp.float32)
    member = (seq_of_shard[None, :] == seq_ids[:, None]).astype(jnp.float32)
    rotated = jnp.einsum("ed,dij->eij", member, received, precision=lax.Precision.HIGHEST)
    scaled = rotated / LEN / (eigvals + damping)[None]
    terms = jnp.einsum(
        "qij,eij->qe", queries.astype(jnp.float32), scaled, precision=lax.Precision.HIGHEST
    )
    return lax.psum(terms, "blk")


def solution(mesh):
    in_specs = (
        P(("grp", "blk"), None),
        P(("grp", "blk"), None),
        P("blk", None),
        P("blk", None),
        P("blk", None),
        P("grp", "blk", None),
        P(),
        P("grp"),
    )
    out_specs = P("grp", None)
    small = mesh.shape["grp"] == 2 and mesh.shape["blk"] == NZ * NY * NC
    return jax.shard_map(fused if small else shards, mesh=mesh, in_specs=in_specs, out_specs=out_specs, check_vma=False)
```

```python
import functools

import jax
import jax.numpy as jnp
from jax import lax
from jax.experimental import pallas as pl
from jax.experimental.pallas import tpu as pltpu
from jax.sharding import PartitionSpec as P

LEN = 2048


damping = 0.1

NZ, NY, NC = 4, 2, 2
ROWS = 16
LANES = 128
MESH = pl.DeviceIdType.MESH


def kernel(
    cuts, fold_s, fold_a, width_s, width_a, nq, seqs,
    owner_ref, seq_ref, basis_a_ref, basis_s_ref, eig_ref, query_ref, acts_ref, grads_ref, out_ref,
    buf, acts_v, grads_v, basis_a_v, basis_s_v, eig_v, query_v, acc_s, rot_a, w_perm, fin,
    load_sem, own_sem, z_send, z_recv, y_send, y_recv, x_send, x_recv, c_send, c_recv, f_send, f_recv,
):
    mine, theirs, shared = cuts
    grp = lax.axis_index("grp")
    me = lax.axis_index("blk")
    core, y, z = me % NC, (me // NC) % NY, me // (NC * NY)
    blocks = NZ * NY * NC
    line = NZ * ROWS
    half = NY * line

    def slot_of(index):
        return (
            (index + core) % NC * (NY * NZ)
            + (index // NC + y) % NY * NZ
            + (index // (NC * NY) + NZ - z) % NZ
        )

    barrier = pltpu.get_barrier_semaphore()
    for step in range(1, blocks):
        pl.semaphore_signal(
            barrier, inc=1, device_id={"blk": lax.rem(me + step, blocks)}, device_id_type=MESH
        )
    pl.semaphore_signal(barrier, inc=1, device_id={"grp": 1 - grp}, device_id_type=MESH)

    own = [
        pltpu.make_async_copy(src, dst, own_sem.at[n])
        for n, (src, dst) in enumerate([
            (basis_s_ref, basis_s_v), (basis_a_ref, basis_a_v), (eig_ref, eig_v), (query_ref, query_v)
        ])
    ]
    loads = [
        pltpu.make_async_copy(
            grads_ref.at[:, pl.ds(g * width_s, width_s)],
            grads_v.at[:, pl.ds(g * width_s, width_s)],
            load_sem.at[1 + g],
        )
        for g in range(fold_s)
    ] + [
        pltpu.make_async_copy(acts_ref, acts_v, load_sem.at[0])
    ]
    for load in own + loads:
        load.start()

    own[0].wait()
    for start in range(0, width_s, width_s // 5):
        width = width_s // 5
        pieces = [basis_s_v[:, pl.ds(g * width_s + start, width)].astype(jnp.float32) for g in range(fold_s)]
        buf[0:ROWS, pl.ds(start, width)] = jnp.concatenate(pieces, axis=0).astype(jnp.bfloat16)
    own[1].wait()
    pieces = [basis_a_v[:, pl.ds(h * width_a, width_a)].astype(jnp.float32) for h in range(fold_a)]
    buf[0:ROWS, pl.ds(width_s, width_a)] = jnp.concatenate(pieces, axis=0).astype(jnp.bfloat16)
    own[2].wait()
    own[3].wait()
    query = query_v[...].astype(jnp.float32)
    pieces = [query[:, i, :] / LEN / (eig_v[i:i + 1, :] + damping) for i in range(query.shape[1])]
    buf[0:ROWS, pl.ds(width_s + width_a, LANES)] = jnp.concatenate(pieces, axis=1).astype(jnp.bfloat16)
    pl.semaphore_wait(barrier, blocks)

    passed = [(pl.multiple_of((grp * len(mine) + n) * w, LANES), w) for n, w in enumerate(mine)]
    passed += shared
    other = [(pl.multiple_of(((1 - grp) * len(theirs) + n) * w, LANES), w) for n, w in enumerate(theirs)]

    sent = []

    def band(row, rows, column):
        start, width = column
        return buf.at[pl.ds(row, rows), pl.ds(start, width)]

    def descriptor(row, to_row, rows, column, send_sem, recv_sem, target):
        return pltpu.make_async_remote_copy(
            src_ref=band(row, rows, column), dst_ref=band(to_row, rows, column),
            send_sem=send_sem, recv_sem=recv_sem, device_id=target, device_id_type=MESH,
        )

    def send(*copy):
        sent.append(descriptor(*copy))
        sent[-1].start()

    def arrived(row, rows, column, recv_sem):
        ref = band(row, rows, column)
        pltpu.make_async_copy(ref, ref, recv_sem).wait()

    to_y = {"blk": (z * NY + 1 - y) * NC + core}
    to_core = {"blk": (z * NY + y) * NC + 1 - core}
    to_x = {"grp": 1 - grp}

    inner = (z == 1) | (z == NZ - 2)
    mate = jnp.where(z < 2, 1 - z, 5 - z)
    across = jnp.where(z < 2, 2, 1)
    near_row = pl.multiple_of((z + NZ - mate) % NZ * ROWS, ROWS)
    far_row = pl.multiple_of((z + NZ - across) % NZ * ROWS, ROWS)
    mate_at = (mate + NZ - z) % NZ
    mate_row = pl.multiple_of(mate_at * ROWS, ROWS)
    relay_row = pl.multiple_of(z * ROWS, ROWS)
    relay_to = pl.multiple_of((NZ - 1 - z) * ROWS, ROWS)
    relayed_row = pl.multiple_of(jnp.where(z == 0, 2, 1) * ROWS, ROWS)

    def to_z(other_z):
        return {"blk": (other_z * NY + y) * NC + core}

    def relay(c):
        return descriptor(
            relay_row, relay_to, 2 * ROWS, passed[c], z_send.at[c, 0], z_recv.at[c, 0], to_z(mate)
        )

    def start(c):
        send(0, near_row, ROWS, passed[c], z_send.at[c, 1], z_recv.at[c, 1], to_z(mate))
        send(0, far_row, ROWS, passed[c], z_send.at[c, 2], z_recv.at[c, 1 + (z + NZ - across) % 2 + 1], to_z(across))
        send(0, line, ROWS, passed[c], y_send.at[c, 0], y_recv.at[c, 0], to_y)

    def z_done(c):
        @pl.when(inner)
        def _():
            for n in range(2):
                row = pl.multiple_of(relay_row + n * ROWS, ROWS)
                arrived(row, ROWS, passed[c], z_recv.at[c, 2 + (z + n) % 2])
            relay(c).start()
        @pl.when(jnp.logical_not(inner))
        def _():
            arrived(relayed_row, 2 * ROWS, passed[c], z_recv.at[c, 0])
        arrived(mate_row, ROWS, passed[c], z_recv.at[c, 1])
        send(ROWS, line + ROWS, line - ROWS, passed[c], y_send.at[c, 1], y_recv.at[c, 1], to_y)
        if c < len(mine):
            send(ROWS, ROWS, line - ROWS, passed[c], x_send.at[c, 0], x_recv.at[c, 0], to_x)

    def y_own(c):
        arrived(line, ROWS, passed[c], y_recv.at[c, 0])
        if c < len(mine):
            send(line, line, ROWS, passed[c], x_send.at[c, 1], x_recv.at[c, 1], to_x)

    def y_done(c):
        arrived(line + ROWS, line - ROWS, passed[c], y_recv.at[c, 1])
        if c < len(mine):
            send(line + ROWS, line + ROWS, line - ROWS, passed[c], x_send.at[c, 2], x_recv.at[c, 2], to_x)
        send(0, half, half, passed[c], c_send.at[c], c_recv.at[c], to_core)

    def x_done(c):
        arrived(ROWS, line - ROWS, other[c], x_recv.at[c, 0])
        arrived(line, ROWS, other[c], x_recv.at[c, 1])
        arrived(line + ROWS, line - ROWS, other[c], x_recv.at[c, 2])
        k = len(passed) + c
        send(0, half, half, other[c], c_send.at[k], c_recv.at[k], to_core)

    first = [True]

    def multiply(column):
        start, width = column
        if first[0]:
            for load in loads:
                load.wait()
            acc_s[...] = jnp.zeros_like(acc_s)
            first[0] = False
        basis = buf[:, pl.ds(start, width)]
        for g in range(fold_s):
            at = pl.multiple_of(g * width_s + start, LANES)
            acc_s[g] += lax.dot_general(
                grads_v[:, pl.ds(at, width)], basis,
                (((1,), (1,)), ((), ())), preferred_element_type=jnp.float32,
            )

    def side():
        tokens, lanes = acts_v.shape[0], blocks * ROWS
        lane = lax.broadcasted_iota(jnp.int32, (tokens, lanes), 1)
        basis = buf[:, pl.ds(width_s, width_a)]
        per = ROWS // fold_a
        total = jnp.zeros((tokens, lanes), jnp.float32)
        for h in range(fold_a):
            part = lax.dot_general(
                acts_v[:, pl.ds(h * width_a, width_a)], basis,
                (((1,), (1,)), ((), ())), preferred_element_type=jnp.float32,
            )
            total += jnp.where((lane % ROWS) // per == h, part, 0.0)
        shift = per
        while shift < ROWS:
            total += pltpu.roll(total, lanes - shift, 1)
            shift *= 2
        row = lax.broadcasted_iota(jnp.int32, (lanes, LANES), 0)
        position = lax.broadcasted_iota(jnp.int32, (lanes, LANES), 1) % (per * blocks)
        place = jnp.zeros((lanes, LANES), jnp.int32)
        for k in range(blocks):
            place = jnp.where(position // per == k, slot_of(owner_ref[k]), place)
        pick = jnp.where(row == place * ROWS + position % per, 1.0, 0.0).astype(jnp.bfloat16)
        rot_a[...] = jnp.dot(
            total.astype(jnp.bfloat16), pick, preferred_element_type=jnp.float32
        ).astype(jnp.bfloat16)
        row = lax.broadcasted_iota(jnp.int32, (lanes, lanes), 0)
        column = lax.broadcasted_iota(jnp.int32, (lanes, lanes), 1)
        place = jnp.zeros((lanes, lanes), jnp.int32)
        for k in range(blocks):
            place = jnp.where(column // ROWS == slot_of(k), slot_of(owner_ref[k]), place)
        move = (row // ROWS == place) & (row % ROWS == column % ROWS)
        w_perm[...] = jnp.dot(
            jnp.where(move, 1.0, 0.0).astype(jnp.bfloat16),
            buf[:, pl.ds(width_s + width_a, LANES)],
            preferred_element_type=jnp.float32,
        )

    def work(k, column):
        arrived(half, half, column, c_recv.at[k])
        if isinstance(column[0], int) and column[0] >= width_s:
            side()
        else:
            multiply(column)

    count, ahead = len(passed), 2
    for c in range(ahead):
        start(c)
    for s in range(count + 4):
        if s + ahead < count:
            start(s + ahead)
        if s < count:
            y_own(s)
            z_done(s)
        if 0 <= s - 1 < count:
            y_done(s - 1)
        if 0 <= s - 2 < len(other):
            x_done(s - 2)
        if 0 <= s - 3 < len(other):
            work(count + s - 3, other[s - 3])
        if 0 <= s - 2 < count:
            work(s - 2, passed[s - 2])

    tokens, lanes = grads_v.shape[0], blocks * ROWS
    per = ROWS // fold_s
    lane = lax.broadcasted_iota(jnp.int32, (tokens, lanes), 1)
    total = jnp.zeros((tokens, lanes), jnp.float32)
    for g in range(fold_s):
        total += jnp.where((lane % ROWS) // per == g, acc_s[g], 0.0)
    shift = per
    while shift < ROWS:
        total += pltpu.roll(total, lanes - shift, 1)
        shift *= 2
    partial = lax.dot_general(
        total.astype(jnp.bfloat16), rot_a[...],
        (((0,), (0,)), ((), ())), preferred_element_type=jnp.float32,
    )
    row = lax.broadcasted_iota(jnp.int32, (lanes, LANES), 0)
    lane = lax.broadcasted_iota(jnp.int32, (lanes, LANES), 1)
    partial = jnp.where(row % ROWS == lane // (LANES // per), partial, 0.0)
    partial = jnp.sum(partial.reshape(blocks, ROWS, LANES), axis=1, keepdims=True)
    terms = jnp.sum(w_perm[...].reshape(blocks, nq, LANES) * partial, axis=0)
    score = jnp.sum(terms, axis=1, keepdims=True)
    row = lax.broadcasted_iota(jnp.int32, (nq, LANES), 0)
    lane = lax.broadcasted_iota(jnp.int32, (nq, LANES), 1)
    seq = seq_ref[me]
    keep = (lane % nq == row) & (lane // nq == seq)
    fin[me] = jnp.sum(jnp.where(keep, score, 0.0), axis=0, keepdims=True)
    for step in range(1, blocks):
        copy = pltpu.make_async_remote_copy(
            src_ref=fin.at[me], dst_ref=fin.at[me],
            send_sem=f_send.at[step - 1], recv_sem=f_recv.at[step - 1],
            device_id={"blk": lax.rem(me + step, blocks)}, device_id_type=MESH,
        )
        copy.start()
        sent.append(copy)
    for step in range(1, blocks):
        part = fin.at[lax.rem(me + blocks - step, blocks)]
        pltpu.make_async_copy(part, part, f_recv.at[step - 1]).wait()
    final = jnp.sum(fin[...], axis=0)
    outs = [final] + [pltpu.roll(final, LANES - e * nq, 1) for e in range(1, seqs)]
    out_ref[...] = jnp.concatenate([out[:, :nq] for out in outs], axis=0)
    for copy in sent:
        copy.wait_send()

    @pl.when(inner)
    def _():
        for c in range(count):
            relay(c).wait_send()


def fused(acts, grads, basis_act, basis_grad, eigvals, queries, owner, seq_of_shard):
    blocks = NZ * NY * NC
    tokens = acts.shape[0]
    nq = queries.shape[0]
    seqs = tokens * blocks // LEN
    fold_a = ROWS // basis_act.shape[0]
    fold_s = ROWS // basis_grad.shape[0]
    width_a = basis_act.shape[1] // fold_a
    width_s = basis_grad.shape[1] // fold_s

    total = width_s + width_a + LANES
    unit = width_s // 10
    mine = [unit] * 4
    shared = [
        (width_s, width_a + LANES),
        (8 * unit, unit),
        (9 * unit, unit),
    ]
    passed = len(mine) + len(shared)
    rows = blocks * ROWS
    dma = pltpu.SemaphoreType.DMA
    vmem = pl.BlockSpec(memory_space=pltpu.VMEM)
    smem = pl.BlockSpec(memory_space=pltpu.SMEM)
    anywhere = pl.BlockSpec(memory_space=pl.ANY)
    return pl.pallas_call(
        functools.partial(
            kernel, (mine, mine, shared), fold_s, fold_a, width_s, width_a, nq, seqs
        ),
        out_shape=jax.ShapeDtypeStruct((seqs, nq), jnp.float32),
        in_specs=[smem, smem] + [anywhere] * 6,
        out_specs=vmem,
        scratch_shapes=[
            pltpu.VMEM((rows, total), jnp.bfloat16),
            pltpu.VMEM(acts.shape, jnp.bfloat16),
            pltpu.VMEM(grads.shape, jnp.bfloat16),
            pltpu.VMEM(basis_act.shape, jnp.bfloat16),
            pltpu.VMEM(basis_grad.shape, jnp.bfloat16),
            pltpu.VMEM(eigvals.shape, jnp.float32),
            pltpu.VMEM(queries.shape, jnp.bfloat16),
            pltpu.VMEM((fold_s, tokens, rows), jnp.float32),
            pltpu.VMEM((tokens, LANES), jnp.bfloat16),
            pltpu.VMEM((rows, LANES), jnp.float32),
            pltpu.VMEM((blocks, 1, LANES), jnp.float32),
            dma((1 + fold_s,)),
            dma((4,)),
            dma((passed, NZ)),
            dma((passed, NZ)),
            dma((passed, 2)),
            dma((passed, 2)),
            dma((len(mine), 3)),
            dma((len(mine), 3)),
            dma((passed + len(mine),)),
            dma((passed + len(mine),)),
            dma((blocks - 1,)),
            dma((blocks - 1,)),
        ],
        compiler_params=pltpu.CompilerParams(
            collective_id=0, has_side_effects=True, vmem_limit_bytes=60 * 1024 * 1024
        ),
    )(owner, seq_of_shard, basis_act, basis_grad, eigvals, queries, acts, grads).T


def reorder(rotated_dev, owner, block):
    width = rotated_dev.shape[1]
    column = jnp.arange(width, dtype=jnp.int32)
    source = owner[column // block] * block + column % block
    return jnp.take(rotated_dev, source, axis=1)


def shards(acts, grads, basis_act, basis_grad, eigvals, queries, owner, seq_of_shard):
    blocks = lax.axis_size("blk")
    block_a = basis_act.shape[0]
    block_s = basis_grad.shape[0]
    rot_a_dev = lax.dot_general(
        acts,
        lax.all_gather(basis_act, "blk", axis=0, tiled=True),
        (((1,), (1,)), ((), ())),
        preferred_element_type=jnp.float32,
    )
    rot_s_dev = lax.dot_general(
        grads,
        lax.all_gather(basis_grad, "blk", axis=0, tiled=True),
        (((1,), (1,)), ((), ())),
        preferred_element_type=jnp.float32,
    )
    rot_a = reorder(rot_a_dev, owner, block_a).astype(jnp.bfloat16)
    rot_s = reorder(rot_s_dev, owner, block_s).astype(jnp.bfloat16)
    partial_grad = lax.dot_general(
        rot_s, rot_a, (((0,), (0,)), ((), ())), preferred_element_type=jnp.float32
    )
    seq_count = acts.shape[0] * blocks // LEN
    seq_ids = jnp.arange(seq_count, dtype=jnp.int32)
    received = lax.all_to_all(
        partial_grad[None].astype(jnp.bfloat16), "blk", split_axis=1, concat_axis=0, tiled=True
    ).astype(jnp.float32)
    member = (seq_of_shard[None, :] == seq_ids[:, None]).astype(jnp.float32)
    rotated = jnp.einsum("ed,dij->eij", member, received, precision=lax.Precision.HIGHEST)
    scaled = rotated / LEN / (eigvals + damping)[None]
    terms = jnp.einsum(
        "qij,eij->qe", queries.astype(jnp.float32), scaled, precision=lax.Precision.HIGHEST
    )
    return lax.psum(terms, "blk")


def solution(mesh):
    in_specs = (
        P(("grp", "blk"), None),
        P(("grp", "blk"), None),
        P("blk", None),
        P("blk", None),
        P("blk", None),
        P("grp", "blk", None),
        P(),
        P("grp"),
    )
    out_specs = P("grp", None)
    small = mesh.shape["grp"] == 2 and mesh.shape["blk"] == NZ * NY * NC
    return jax.shard_map(fused if small else shards, mesh=mesh, in_specs=in_specs, out_specs=out_specs, check_vma=False)
```

```python
import functools

import jax
import jax.numpy as jnp
from jax import lax
from jax.experimental import pallas as pl
from jax.experimental.pallas import tpu as pltpu
from jax.sharding import PartitionSpec as P

LEN = 2048


damping = 0.1

NZ, NY, NC = 4, 2, 2
ROWS = 16
LANES = 128
MESH = pl.DeviceIdType.MESH


def order(mine, passed, total, hop, turn, step, unit):
    cost = [unit * width / total for width in passed]
    arrive, y_free, x_items, events = [], sum(cost), [], []
    done, ready = 0.0, []
    for c, t in enumerate(cost):
        done += t
        arrive.append(step + 4 * done)
        events.append((hop + done, "y_own", c))
        events.append((arrive[c], "z_done", c))
        y_free = max(y_free, arrive[c]) + 3 * t
        ready.append(y_free + hop)
        events.append((ready[c], "y_done", c))
        events.append((ready[c] + turn, "passed", c))
        if c < mine:
            x_items += [(hop + done, t, c), (arrive[c], 3 * t, c), (ready[c], 3 * t, c)]
    x_free, last = 0.0, [0.0] * mine
    for start, t, c in sorted(x_items):
        x_free = max(x_free, start) + t
        last[c] = x_free + hop
    for c in range(mine):
        events.append((last[c], "x_done", c))
        events.append((last[c] + turn, "other", c))
    return [event[1:] for event in sorted(events)]


def kernel(
    cuts, fold_s, fold_a, width_s, width_a, nq, seqs,
    owner_ref, seq_ref, basis_a_ref, basis_s_ref, eig_ref, query_ref, acts_ref, grads_ref, out_ref,
    buf, acts_v, grads_v, basis_a_v, basis_s_v, eig_v, query_v, acc_s, rot_a, w_perm, fin,
    load_sem, own_sem, z_send, z_recv, y_send, y_recv, x_send, x_recv, c_send, c_recv, f_send, f_recv,
):
    mine, shared = cuts
    grp = lax.axis_index("grp")
    me = lax.axis_index("blk")
    core, y, z = me % NC, (me // NC) % NY, me // (NC * NY)
    blocks = NZ * NY * NC
    line = NZ * ROWS
    half = NY * line

    def slot_of(index):
        return (
            (index + core) % NC * (NY * NZ)
            + (index // NC + y) % NY * NZ
            + (index // (NC * NY) + NZ - z) % NZ
        )

    barrier = pltpu.get_barrier_semaphore()
    for step in range(1, blocks):
        pl.semaphore_signal(
            barrier, inc=1, device_id={"blk": lax.rem(me + step, blocks)}, device_id_type=MESH
        )
    pl.semaphore_signal(barrier, inc=1, device_id={"grp": 1 - grp}, device_id_type=MESH)

    own = [
        pltpu.make_async_copy(src, dst, own_sem.at[n])
        for n, (src, dst) in enumerate([
            (basis_s_ref, basis_s_v), (basis_a_ref, basis_a_v), (eig_ref, eig_v), (query_ref, query_v)
        ])
    ]
    loads = [
        pltpu.make_async_copy(
            grads_ref.at[:, pl.ds(g * width_s, width_s)],
            grads_v.at[:, pl.ds(g * width_s, width_s)],
            load_sem.at[1 + g],
        )
        for g in range(fold_s)
    ] + [
        pltpu.make_async_copy(acts_ref, acts_v, load_sem.at[0])
    ]
    for load in own + loads:
        load.start()

    own[0].wait()
    for start in range(0, width_s, width_s // 5):
        width = width_s // 5
        pieces = [basis_s_v[:, pl.ds(g * width_s + start, width)].astype(jnp.float32) for g in range(fold_s)]
        buf[0:ROWS, pl.ds(start, width)] = jnp.concatenate(pieces, axis=0).astype(jnp.bfloat16)
    own[1].wait()
    pieces = [basis_a_v[:, pl.ds(h * width_a, width_a)].astype(jnp.float32) for h in range(fold_a)]
    buf[0:ROWS, pl.ds(width_s, width_a)] = jnp.concatenate(pieces, axis=0).astype(jnp.bfloat16)
    own[2].wait()
    own[3].wait()
    query = query_v[...].astype(jnp.float32)
    pieces = [query[:, i, :] / LEN / (eig_v[i:i + 1, :] + damping) for i in range(query.shape[1])]
    buf[0:ROWS, pl.ds(width_s + width_a, LANES)] = jnp.concatenate(pieces, axis=1).astype(jnp.bfloat16)
    pl.semaphore_wait(barrier, blocks)

    def columns(plane):
        return [(pl.multiple_of(plane * sum(mine) + sum(mine[:n]), LANES), w) for n, w in enumerate(mine)]

    passed = columns(grp) + shared
    other = columns(1 - grp)

    sent = []

    def band(row, rows, column):
        start, width = column
        return buf.at[pl.ds(row, rows), pl.ds(start, width)]

    def descriptor(row, to_row, rows, column, send_sem, recv_sem, target):
        return pltpu.make_async_remote_copy(
            src_ref=band(row, rows, column), dst_ref=band(to_row, rows, column),
            send_sem=send_sem, recv_sem=recv_sem, device_id=target, device_id_type=MESH,
        )

    def send(*copy):
        sent.append(descriptor(*copy))
        sent[-1].start()

    def arrived(row, rows, column, recv_sem):
        ref = band(row, rows, column)
        pltpu.make_async_copy(ref, ref, recv_sem).wait()

    to_y = {"blk": (z * NY + 1 - y) * NC + core}
    to_core = {"blk": (z * NY + y) * NC + 1 - core}
    to_x = {"grp": 1 - grp}

    def start(c):
        for step in (2, 1, 3):
            to_z = {"blk": lax.rem(me + step * NY * NC, blocks)}
            send(
                0, (NZ - step) * ROWS, ROWS, passed[c],
                z_send.at[c, step], z_recv.at[c, NZ - step], to_z,
            )
        send(0, line, ROWS, passed[c], y_send.at[c, 0], y_recv.at[c, 0], to_y)

    def z_done(c):
        for at in range(1, NZ):
            arrived(at * ROWS, ROWS, passed[c], z_recv.at[c, at])
        send(ROWS, line + ROWS, line - ROWS, passed[c], y_send.at[c, 1], y_recv.at[c, 1], to_y)
        if c < len(mine):
            send(ROWS, ROWS, line - ROWS, passed[c], x_send.at[c, 0], x_recv.at[c, 0], to_x)

    def y_own(c):
        arrived(line, ROWS, passed[c], y_recv.at[c, 0])
        if c < len(mine):
            send(line, line, ROWS, passed[c], x_send.at[c, 1], x_recv.at[c, 1], to_x)

    def y_done(c):
        arrived(line + ROWS, line - ROWS, passed[c], y_recv.at[c, 1])
        if c < len(mine):
            send(line + ROWS, line + ROWS, line - ROWS, passed[c], x_send.at[c, 2], x_recv.at[c, 2], to_x)
        send(0, half, half, passed[c], c_send.at[c], c_recv.at[c], to_core)

    def x_done(c):
        arrived(ROWS, line - ROWS, other[c], x_recv.at[c, 0])
        arrived(line, ROWS, other[c], x_recv.at[c, 1])
        arrived(line + ROWS, line - ROWS, other[c], x_recv.at[c, 2])
        k = len(passed) + c
        send(0, half, half, other[c], c_send.at[k], c_recv.at[k], to_core)

    first = [True]

    def multiply(column):
        start, width = column
        if first[0]:
            for load in loads:
                load.wait()
            acc_s[...] = jnp.zeros_like(acc_s)
            first[0] = False
        basis = buf[:, pl.ds(start, width)]
        for g in range(fold_s):
            at = pl.multiple_of(g * width_s + start, LANES)
            acc_s[g] += lax.dot_general(
                grads_v[:, pl.ds(at, width)], basis,
                (((1,), (1,)), ((), ())), preferred_element_type=jnp.float32,
            )

    def side():
        tokens, lanes = acts_v.shape[0], blocks * ROWS
        lane = lax.broadcasted_iota(jnp.int32, (tokens, lanes), 1)
        basis = buf[:, pl.ds(width_s, width_a)]
        per = ROWS // fold_a
        total = jnp.zeros((tokens, lanes), jnp.float32)
        for h in range(fold_a):
            part = lax.dot_general(
                acts_v[:, pl.ds(h * width_a, width_a)], basis,
                (((1,), (1,)), ((), ())), preferred_element_type=jnp.float32,
            )
            total += jnp.where((lane % ROWS) // per == h, part, 0.0)
        shift = per
        while shift < ROWS:
            total += pltpu.roll(total, lanes - shift, 1)
            shift *= 2
        row = lax.broadcasted_iota(jnp.int32, (lanes, LANES), 0)
        position = lax.broadcasted_iota(jnp.int32, (lanes, LANES), 1) % (per * blocks)
        place = jnp.zeros((lanes, LANES), jnp.int32)
        for k in range(blocks):
            place = jnp.where(position // per == k, slot_of(owner_ref[k]), place)
        pick = jnp.where(row == place * ROWS + position % per, 1.0, 0.0).astype(jnp.bfloat16)
        rot_a[...] = jnp.dot(
            total.astype(jnp.bfloat16), pick, preferred_element_type=jnp.float32
        ).astype(jnp.bfloat16)
        row = lax.broadcasted_iota(jnp.int32, (lanes, lanes), 0)
        column = lax.broadcasted_iota(jnp.int32, (lanes, lanes), 1)
        place = jnp.zeros((lanes, lanes), jnp.int32)
        for k in range(blocks):
            place = jnp.where(column // ROWS == slot_of(k), slot_of(owner_ref[k]), place)
        move = (row // ROWS == place) & (row % ROWS == column % ROWS)
        w_perm[...] = jnp.dot(
            jnp.where(move, 1.0, 0.0).astype(jnp.bfloat16),
            buf[:, pl.ds(width_s + width_a, LANES)],
            preferred_element_type=jnp.float32,
        )

    def work(k, column):
        arrived(half, half, column, c_recv.at[k])
        if isinstance(column[0], int) and column[0] >= width_s:
            side()
        else:
            multiply(column)

    count = len(passed)
    for c in range(count):
        start(c)
    actions = {
        "y_own": y_own, "z_done": z_done, "y_done": y_done, "x_done": x_done,
        "passed": lambda c: work(c, passed[c]),
        "other": lambda c: work(count + c, other[c]),
    }
    widths = [width for _, width in passed]
    for action, c in order(len(mine), widths, width_s + width_a + LANES, 3.0, 1.5, 3.0, 4.5):
        actions[action](c)

    tokens, lanes = grads_v.shape[0], blocks * ROWS
    per = ROWS // fold_s
    lane = lax.broadcasted_iota(jnp.int32, (tokens, lanes), 1)
    total = jnp.zeros((tokens, lanes), jnp.float32)
    for g in range(fold_s):
        total += jnp.where((lane % ROWS) // per == g, acc_s[g], 0.0)
    shift = per
    while shift < ROWS:
        total += pltpu.roll(total, lanes - shift, 1)
        shift *= 2
    partial = lax.dot_general(
        total.astype(jnp.bfloat16), rot_a[...],
        (((0,), (0,)), ((), ())), preferred_element_type=jnp.float32,
    )
    row = lax.broadcasted_iota(jnp.int32, (lanes, LANES), 0)
    lane = lax.broadcasted_iota(jnp.int32, (lanes, LANES), 1)
    partial = jnp.where(row % ROWS == lane // (LANES // per), partial, 0.0)
    partial = jnp.sum(partial.reshape(blocks, ROWS, LANES), axis=1, keepdims=True)
    terms = jnp.sum(w_perm[...].reshape(blocks, nq, LANES) * partial, axis=0)
    score = jnp.sum(terms, axis=1, keepdims=True)
    row = lax.broadcasted_iota(jnp.int32, (nq, LANES), 0)
    lane = lax.broadcasted_iota(jnp.int32, (nq, LANES), 1)
    seq = seq_ref[me]
    keep = (lane % nq == row) & (lane // nq == seq)
    fin[me] = jnp.sum(jnp.where(keep, score, 0.0), axis=0, keepdims=True)
    for step in range(1, blocks):
        copy = pltpu.make_async_remote_copy(
            src_ref=fin.at[me], dst_ref=fin.at[me],
            send_sem=f_send.at[step - 1], recv_sem=f_recv.at[step - 1],
            device_id={"blk": lax.rem(me + step, blocks)}, device_id_type=MESH,
        )
        copy.start()
        sent.append(copy)
    for step in range(1, blocks):
        part = fin.at[lax.rem(me + blocks - step, blocks)]
        pltpu.make_async_copy(part, part, f_recv.at[step - 1]).wait()
    final = jnp.sum(fin[...], axis=0)
    outs = [final] + [pltpu.roll(final, LANES - e * nq, 1) for e in range(1, seqs)]
    out_ref[...] = jnp.concatenate([out[:, :nq] for out in outs], axis=0)
    for copy in sent:
        copy.wait_send()


def fused(acts, grads, basis_act, basis_grad, eigvals, queries, owner, seq_of_shard):
    blocks = NZ * NY * NC
    tokens = acts.shape[0]
    nq = queries.shape[0]
    seqs = tokens * blocks // LEN
    fold_a = ROWS // basis_act.shape[0]
    fold_s = ROWS // basis_grad.shape[0]
    width_a = basis_act.shape[1] // fold_a
    width_s = basis_grad.shape[1] // fold_s

    total = width_s + width_a + LANES
    unit = width_s // 10
    mine = [unit] * 4
    shared = [
        (width_s, width_a + LANES),
        (8 * unit, unit), (9 * unit, unit),
    ]
    passed = len(mine) + len(shared)
    rows = blocks * ROWS
    dma = pltpu.SemaphoreType.DMA
    vmem = pl.BlockSpec(memory_space=pltpu.VMEM)
    smem = pl.BlockSpec(memory_space=pltpu.SMEM)
    anywhere = pl.BlockSpec(memory_space=pl.ANY)
    return pl.pallas_call(
        functools.partial(
            kernel, (mine, shared), fold_s, fold_a, width_s, width_a, nq, seqs
        ),
        out_shape=jax.ShapeDtypeStruct((seqs, nq), jnp.float32),
        in_specs=[smem, smem] + [anywhere] * 6,
        out_specs=vmem,
        scratch_shapes=[
            pltpu.VMEM((rows, total), jnp.bfloat16),
            pltpu.VMEM(acts.shape, jnp.bfloat16),
            pltpu.VMEM(grads.shape, jnp.bfloat16),
            pltpu.VMEM(basis_act.shape, jnp.bfloat16),
            pltpu.VMEM(basis_grad.shape, jnp.bfloat16),
            pltpu.VMEM(eigvals.shape, jnp.float32),
            pltpu.VMEM(queries.shape, jnp.bfloat16),
            pltpu.VMEM((fold_s, tokens, rows), jnp.float32),
            pltpu.VMEM((tokens, LANES), jnp.bfloat16),
            pltpu.VMEM((rows, LANES), jnp.float32),
            pltpu.VMEM((blocks, 1, LANES), jnp.float32),
            dma((1 + fold_s,)),
            dma((4,)),
            dma((passed, NZ)),
            dma((passed, NZ)),
            dma((passed, 2)),
            dma((passed, 2)),
            dma((len(mine), 3)),
            dma((len(mine), 3)),
            dma((passed + len(mine),)),
            dma((passed + len(mine),)),
            dma((blocks - 1,)),
            dma((blocks - 1,)),
        ],
        compiler_params=pltpu.CompilerParams(
            collective_id=0, has_side_effects=True, vmem_limit_bytes=60 * 1024 * 1024
        ),
    )(owner, seq_of_shard, basis_act, basis_grad, eigvals, queries, acts, grads).T


def reorder(rotated_dev, owner, block):
    width = rotated_dev.shape[1]
    column = jnp.arange(width, dtype=jnp.int32)
    source = owner[column // block] * block + column % block
    return jnp.take(rotated_dev, source, axis=1)


def shards(acts, grads, basis_act, basis_grad, eigvals, queries, owner, seq_of_shard):
    blocks = lax.axis_size("blk")
    block_a = basis_act.shape[0]
    block_s = basis_grad.shape[0]
    rot_a_dev = lax.dot_general(
        acts,
        lax.all_gather(basis_act, "blk", axis=0, tiled=True),
        (((1,), (1,)), ((), ())),
        preferred_element_type=jnp.float32,
    )
    rot_s_dev = lax.dot_general(
        grads,
        lax.all_gather(basis_grad, "blk", axis=0, tiled=True),
        (((1,), (1,)), ((), ())),
        preferred_element_type=jnp.float32,
    )
    rot_a = reorder(rot_a_dev, owner, block_a).astype(jnp.bfloat16)
    rot_s = reorder(rot_s_dev, owner, block_s).astype(jnp.bfloat16)
    partial_grad = lax.dot_general(
        rot_s, rot_a, (((0,), (0,)), ((), ())), preferred_element_type=jnp.float32
    )
    seq_count = acts.shape[0] * blocks // LEN
    seq_ids = jnp.arange(seq_count, dtype=jnp.int32)
    received = lax.all_to_all(
        partial_grad[None].astype(jnp.bfloat16), "blk", split_axis=1, concat_axis=0, tiled=True
    ).astype(jnp.float32)
    member = (seq_of_shard[None, :] == seq_ids[:, None]).astype(jnp.float32)
    rotated = jnp.einsum("ed,dij->eij", member, received, precision=lax.Precision.HIGHEST)
    scaled = rotated / LEN / (eigvals + damping)[None]
    terms = jnp.einsum(
        "qij,eij->qe", queries.astype(jnp.float32), scaled, precision=lax.Precision.HIGHEST
    )
    return lax.psum(terms, "blk")


def solution(mesh):
    in_specs = (
        P(("grp", "blk"), None),
        P(("grp", "blk"), None),
        P("blk", None),
        P("blk", None),
        P("blk", None),
        P("grp", "blk", None),
        P(),
        P("grp"),
    )
    out_specs = P("grp", None)
    small = mesh.shape["grp"] == 2 and mesh.shape["blk"] == NZ * NY * NC
    return jax.shard_map(fused if small else shards, mesh=mesh, in_specs=in_specs, out_specs=out_specs, check_vma=False)
```

```python
import functools

import jax
import jax.numpy as jnp
from jax import lax
from jax.experimental import pallas as pl
from jax.experimental.pallas import tpu as pltpu
from jax.sharding import PartitionSpec as P

LEN = 2048


damping = 0.1

NZ, NY, NC = 4, 2, 2
ROWS = 16
LANES = 128
MESH = pl.DeviceIdType.MESH


def order(mine, passed, total, hop, turn, step, unit):
    cost = [unit * width / total for width in passed]
    arrive, y_free, x_items, events = [], sum(cost), [], []
    done, ready = 0.0, []
    for c, t in enumerate(cost):
        done += t
        arrive.append(step + 4 * done)
        events.append((hop + done, "y_own", c))
        events.append((arrive[c], "z_done", c))
        y_free = max(y_free, arrive[c]) + 3 * t
        ready.append(y_free + hop)
        events.append((ready[c], "y_done", c))
        events.append((ready[c] + turn, "passed", c))
        if c < mine:
            x_items += [(hop + done, t, c), (arrive[c], 3 * t, c), (ready[c], 3 * t, c)]
    x_free, last = 0.0, [0.0] * mine
    for start, t, c in sorted(x_items):
        x_free = max(x_free, start) + t
        last[c] = x_free + hop
    for c in range(mine):
        events.append((last[c], "x_done", c))
        events.append((last[c] + turn, "other", c))
    return [event[1:] for event in sorted(events)]


def kernel(
    cuts, fold_s, fold_a, width_s, width_a, nq, seqs,
    owner_ref, seq_ref, basis_a_ref, basis_s_ref, eig_ref, query_ref, acts_ref, grads_ref, out_ref,
    buf, acts_v, grads_v, basis_a_v, basis_s_v, eig_v, query_v, acc_s, rot_a, w_perm, fin,
    load_sem, own_sem, z_send, z_recv, y_send, y_recv, x_send, x_recv, c_send, c_recv, f_send, f_recv,
):
    mine, shared = cuts
    grp = lax.axis_index("grp")
    me = lax.axis_index("blk")
    core, y, z = me % NC, (me // NC) % NY, me // (NC * NY)
    blocks = NZ * NY * NC
    line = NZ * ROWS
    half = NY * line

    def slot_of(index):
        return (
            (index + core) % NC * (NY * NZ)
            + (index // NC + y) % NY * NZ
            + (index // (NC * NY) + NZ - z) % NZ
        )

    barrier = pltpu.get_barrier_semaphore()
    for step in range(1, blocks):
        pl.semaphore_signal(
            barrier, inc=1, device_id={"blk": lax.rem(me + step, blocks)}, device_id_type=MESH
        )
    pl.semaphore_signal(barrier, inc=1, device_id={"grp": 1 - grp}, device_id_type=MESH)

    own = [
        pltpu.make_async_copy(src, dst, own_sem.at[n])
        for n, (src, dst) in enumerate([
            (basis_s_ref, basis_s_v), (basis_a_ref, basis_a_v), (eig_ref, eig_v), (query_ref, query_v)
        ])
    ]
    loads = [
        pltpu.make_async_copy(
            grads_ref.at[:, pl.ds(g * width_s, width_s)],
            grads_v.at[:, pl.ds(g * width_s, width_s)],
            load_sem.at[1 + g],
        )
        for g in range(fold_s)
    ] + [
        pltpu.make_async_copy(acts_ref, acts_v, load_sem.at[0])
    ]
    for load in own + loads:
        load.start()

    own[0].wait()
    for start in range(0, width_s, width_s // 5):
        width = width_s // 5
        pieces = [basis_s_v[:, pl.ds(g * width_s + start, width)].astype(jnp.float32) for g in range(fold_s)]
        buf[0:ROWS, pl.ds(start, width)] = jnp.concatenate(pieces, axis=0).astype(jnp.bfloat16)
    own[1].wait()
    pieces = [basis_a_v[:, pl.ds(h * width_a, width_a)].astype(jnp.float32) for h in range(fold_a)]
    buf[0:ROWS, pl.ds(width_s, width_a)] = jnp.concatenate(pieces, axis=0).astype(jnp.bfloat16)
    own[2].wait()
    own[3].wait()
    query = query_v[...].astype(jnp.float32)
    pieces = [query[:, i, :] / LEN / (eig_v[i:i + 1, :] + damping) for i in range(query.shape[1])]
    buf[0:ROWS, pl.ds(width_s + width_a, LANES)] = jnp.concatenate(pieces, axis=1).astype(jnp.bfloat16)
    pl.semaphore_wait(barrier, blocks)

    def columns(plane):
        return [(pl.multiple_of(plane * sum(mine) + sum(mine[:n]), LANES), w) for n, w in enumerate(mine)]

    passed = columns(grp) + shared
    other = columns(1 - grp)

    sent = []

    def band(row, rows, column):
        start, width = column
        return buf.at[pl.ds(row, rows), pl.ds(start, width)]

    def descriptor(row, to_row, rows, column, send_sem, recv_sem, target):
        return pltpu.make_async_remote_copy(
            src_ref=band(row, rows, column), dst_ref=band(to_row, rows, column),
            send_sem=send_sem, recv_sem=recv_sem, device_id=target, device_id_type=MESH,
        )

    def send(*copy):
        sent.append(descriptor(*copy))
        sent[-1].start()

    def arrived(row, rows, column, recv_sem):
        ref = band(row, rows, column)
        pltpu.make_async_copy(ref, ref, recv_sem).wait()

    to_y = {"blk": (z * NY + 1 - y) * NC + core}
    to_core = {"blk": (z * NY + y) * NC + 1 - core}
    to_x = {"grp": 1 - grp}

    def start(c):
        for step in (2, 1, 3):
            to_z = {"blk": lax.rem(me + step * NY * NC, blocks)}
            send(
                0, (NZ - step) * ROWS, ROWS, passed[c],
                z_send.at[c, step], z_recv.at[c, NZ - step], to_z,
            )
        send(0, line, ROWS, passed[c], y_send.at[c, 0], y_recv.at[c, 0], to_y)

    def z_done(c):
        for at in range(1, NZ):
            arrived(at * ROWS, ROWS, passed[c], z_recv.at[c, at])
        send(ROWS, line + ROWS, line - ROWS, passed[c], y_send.at[c, 1], y_recv.at[c, 1], to_y)
        if c < len(mine):
            send(ROWS, ROWS, line - ROWS, passed[c], x_send.at[c, 0], x_recv.at[c, 0], to_x)

    def y_own(c):
        arrived(line, ROWS, passed[c], y_recv.at[c, 0])
        if c < len(mine):
            send(line, line, ROWS, passed[c], x_send.at[c, 1], x_recv.at[c, 1], to_x)

    def y_done(c):
        arrived(line + ROWS, line - ROWS, passed[c], y_recv.at[c, 1])
        if c < len(mine):
            send(line + ROWS, line + ROWS, line - ROWS, passed[c], x_send.at[c, 2], x_recv.at[c, 2], to_x)
        send(0, half, half, passed[c], c_send.at[c], c_recv.at[c], to_core)

    def x_done(c):
        arrived(ROWS, line - ROWS, other[c], x_recv.at[c, 0])
        arrived(line, ROWS, other[c], x_recv.at[c, 1])
        arrived(line + ROWS, line - ROWS, other[c], x_recv.at[c, 2])
        k = len(passed) + c
        send(0, half, half, other[c], c_send.at[k], c_recv.at[k], to_core)

    first = [True]

    def multiply(column):
        start, width = column
        if first[0]:
            for load in loads:
                load.wait()
            acc_s[...] = jnp.zeros_like(acc_s)
            first[0] = False
        basis = buf[:, pl.ds(start, width)]
        for g in range(fold_s):
            at = pl.multiple_of(g * width_s + start, LANES)
            acc_s[g] += lax.dot_general(
                grads_v[:, pl.ds(at, width)], basis,
                (((1,), (1,)), ((), ())), preferred_element_type=jnp.float32,
            )

    def side():
        tokens, lanes = acts_v.shape[0], blocks * ROWS
        lane = lax.broadcasted_iota(jnp.int32, (tokens, lanes), 1)
        basis = buf[:, pl.ds(width_s, width_a)]
        per = ROWS // fold_a
        total = jnp.zeros((tokens, lanes), jnp.float32)
        for h in range(fold_a):
            part = lax.dot_general(
                acts_v[:, pl.ds(h * width_a, width_a)], basis,
                (((1,), (1,)), ((), ())), preferred_element_type=jnp.float32,
            )
            total += jnp.where((lane % ROWS) // per == h, part, 0.0)
        shift = per
        while shift < ROWS:
            total += pltpu.roll(total, lanes - shift, 1)
            shift *= 2
        row = lax.broadcasted_iota(jnp.int32, (lanes, LANES), 0)
        position = lax.broadcasted_iota(jnp.int32, (lanes, LANES), 1) % (per * blocks)
        place = jnp.zeros((lanes, LANES), jnp.int32)
        for k in range(blocks):
            place = jnp.where(position // per == k, slot_of(owner_ref[k]), place)
        pick = jnp.where(row == place * ROWS + position % per, 1.0, 0.0).astype(jnp.bfloat16)
        rot_a[...] = jnp.dot(
            total.astype(jnp.bfloat16), pick, preferred_element_type=jnp.float32
        ).astype(jnp.bfloat16)
        row = lax.broadcasted_iota(jnp.int32, (lanes, lanes), 0)
        column = lax.broadcasted_iota(jnp.int32, (lanes, lanes), 1)
        place = jnp.zeros((lanes, lanes), jnp.int32)
        for k in range(blocks):
            place = jnp.where(column // ROWS == slot_of(k), slot_of(owner_ref[k]), place)
        move = (row // ROWS == place) & (row % ROWS == column % ROWS)
        w_perm[...] = jnp.dot(
            jnp.where(move, 1.0, 0.0).astype(jnp.bfloat16),
            buf[:, pl.ds(width_s + width_a, LANES)],
            preferred_element_type=jnp.float32,
        )

    def work(k, column):
        arrived(half, half, column, c_recv.at[k])
        if isinstance(column[0], int) and column[0] >= width_s:
            side()
        else:
            multiply(column)

    count = len(passed)
    for c in range(count):
        start(c)
    actions = {
        "y_own": y_own, "z_done": z_done, "y_done": y_done, "x_done": x_done,
        "passed": lambda c: work(c, passed[c]),
        "other": lambda c: work(count + c, other[c]),
    }
    widths = [width for _, width in passed]
    for action, c in order(len(mine), widths, width_s + width_a + LANES, 3.0, 1.5, 3.0, 4.5):
        actions[action](c)

    tokens, lanes = grads_v.shape[0], blocks * ROWS
    per = ROWS // fold_s
    lane = lax.broadcasted_iota(jnp.int32, (tokens, lanes), 1)
    total = jnp.zeros((tokens, lanes), jnp.float32)
    for g in range(fold_s):
        total += jnp.where((lane % ROWS) // per == g, acc_s[g], 0.0)
    shift = per
    while shift < ROWS:
        total += pltpu.roll(total, lanes - shift, 1)
        shift *= 2
    partial = lax.dot_general(
        total.astype(jnp.bfloat16), rot_a[...],
        (((0,), (0,)), ((), ())), preferred_element_type=jnp.float32,
    )
    row = lax.broadcasted_iota(jnp.int32, (lanes, LANES), 0)
    lane = lax.broadcasted_iota(jnp.int32, (lanes, LANES), 1)
    partial = jnp.where(row % ROWS == lane // (LANES // per), partial, 0.0)
    partial = jnp.sum(partial.reshape(blocks, ROWS, LANES), axis=1, keepdims=True)
    terms = jnp.sum(w_perm[...].reshape(blocks, nq, LANES) * partial, axis=0)
    score = jnp.sum(terms, axis=1, keepdims=True)
    row = lax.broadcasted_iota(jnp.int32, (nq, LANES), 0)
    lane = lax.broadcasted_iota(jnp.int32, (nq, LANES), 1)
    seq = seq_ref[me]
    keep = (lane % nq == row) & (lane // nq == seq)
    fin[me] = jnp.sum(jnp.where(keep, score, 0.0), axis=0, keepdims=True)
    for step in range(1, blocks):
        copy = pltpu.make_async_remote_copy(
            src_ref=fin.at[me], dst_ref=fin.at[me],
            send_sem=f_send.at[step - 1], recv_sem=f_recv.at[step - 1],
            device_id={"blk": lax.rem(me + step, blocks)}, device_id_type=MESH,
        )
        copy.start()
        sent.append(copy)
    for copy in sent:
        copy.wait_send()
    for step in range(1, blocks):
        part = fin.at[lax.rem(me + blocks - step, blocks)]
        pltpu.make_async_copy(part, part, f_recv.at[step - 1]).wait()
    final = jnp.sum(fin[...], axis=0)
    outs = [final] + [pltpu.roll(final, LANES - e * nq, 1) for e in range(1, seqs)]
    out_ref[...] = jnp.concatenate([out[:, :nq] for out in outs], axis=0)


def fused(acts, grads, basis_act, basis_grad, eigvals, queries, owner, seq_of_shard):
    blocks = NZ * NY * NC
    tokens = acts.shape[0]
    nq = queries.shape[0]
    seqs = tokens * blocks // LEN
    fold_a = ROWS // basis_act.shape[0]
    fold_s = ROWS // basis_grad.shape[0]
    width_a = basis_act.shape[1] // fold_a
    width_s = basis_grad.shape[1] // fold_s

    total = width_s + width_a + LANES
    unit = width_s // 10
    mine = [unit] * 4
    shared = [
        (width_s, width_a + LANES),
        (8 * unit, unit), (9 * unit, unit),
    ]
    passed = len(mine) + len(shared)
    rows = blocks * ROWS
    dma = pltpu.SemaphoreType.DMA
    vmem = pl.BlockSpec(memory_space=pltpu.VMEM)
    smem = pl.BlockSpec(memory_space=pltpu.SMEM)
    anywhere = pl.BlockSpec(memory_space=pl.ANY)
    return pl.pallas_call(
        functools.partial(
            kernel, (mine, shared), fold_s, fold_a, width_s, width_a, nq, seqs
        ),
        out_shape=jax.ShapeDtypeStruct((seqs, nq), jnp.float32),
        in_specs=[smem, smem] + [anywhere] * 6,
        out_specs=vmem,
        scratch_shapes=[
            pltpu.VMEM((rows, total), jnp.bfloat16),
            pltpu.VMEM(acts.shape, jnp.bfloat16),
            pltpu.VMEM(grads.shape, jnp.bfloat16),
            pltpu.VMEM(basis_act.shape, jnp.bfloat16),
            pltpu.VMEM(basis_grad.shape, jnp.bfloat16),
            pltpu.VMEM(eigvals.shape, jnp.float32),
            pltpu.VMEM(queries.shape, jnp.bfloat16),
            pltpu.VMEM((fold_s, tokens, rows), jnp.float32),
            pltpu.VMEM((tokens, LANES), jnp.bfloat16),
            pltpu.VMEM((rows, LANES), jnp.float32),
            pltpu.VMEM((blocks, 1, LANES), jnp.float32),
            dma((1 + fold_s,)),
            dma((4,)),
            dma((passed, NZ)),
            dma((passed, NZ)),
            dma((passed, 2)),
            dma((passed, 2)),
            dma((len(mine), 3)),
            dma((len(mine), 3)),
            dma((passed + len(mine),)),
            dma((passed + len(mine),)),
            dma((blocks - 1,)),
            dma((blocks - 1,)),
        ],
        compiler_params=pltpu.CompilerParams(
            collective_id=0, has_side_effects=True, vmem_limit_bytes=60 * 1024 * 1024
        ),
    )(owner, seq_of_shard, basis_act, basis_grad, eigvals, queries, acts, grads).T


def reorder(rotated_dev, owner, block):
    width = rotated_dev.shape[1]
    column = jnp.arange(width, dtype=jnp.int32)
    source = owner[column // block] * block + column % block
    return jnp.take(rotated_dev, source, axis=1)


def shards(acts, grads, basis_act, basis_grad, eigvals, queries, owner, seq_of_shard):
    blocks = lax.axis_size("blk")
    block_a = basis_act.shape[0]
    block_s = basis_grad.shape[0]
    rot_a_dev = lax.dot_general(
        acts,
        lax.all_gather(basis_act, "blk", axis=0, tiled=True),
        (((1,), (1,)), ((), ())),
        preferred_element_type=jnp.float32,
    )
    rot_s_dev = lax.dot_general(
        grads,
        lax.all_gather(basis_grad, "blk", axis=0, tiled=True),
        (((1,), (1,)), ((), ())),
        preferred_element_type=jnp.float32,
    )
    rot_a = reorder(rot_a_dev, owner, block_a).astype(jnp.bfloat16)
    rot_s = reorder(rot_s_dev, owner, block_s).astype(jnp.bfloat16)
    partial_grad = lax.dot_general(
        rot_s, rot_a, (((0,), (0,)), ((), ())), preferred_element_type=jnp.float32
    )
    seq_count = acts.shape[0] * blocks // LEN
    seq_ids = jnp.arange(seq_count, dtype=jnp.int32)
    received = lax.all_to_all(
        partial_grad[None].astype(jnp.bfloat16), "blk", split_axis=1, concat_axis=0, tiled=True
    ).astype(jnp.float32)
    member = (seq_of_shard[None, :] == seq_ids[:, None]).astype(jnp.float32)
    rotated = jnp.einsum("ed,dij->eij", member, received, precision=lax.Precision.HIGHEST)
    scaled = rotated / LEN / (eigvals + damping)[None]
    terms = jnp.einsum(
        "qij,eij->qe", queries.astype(jnp.float32), scaled, precision=lax.Precision.HIGHEST
    )
    return lax.psum(terms, "blk")


def solution(mesh):
    in_specs = (
        P(("grp", "blk"), None),
        P(("grp", "blk"), None),
        P("blk", None),
        P("blk", None),
        P("blk", None),
        P("grp", "blk", None),
        P(),
        P("grp"),
    )
    out_specs = P("grp", None)
    small = mesh.shape["grp"] == 2 and mesh.shape["blk"] == NZ * NY * NC
    return jax.shard_map(fused if small else shards, mesh=mesh, in_specs=in_specs, out_specs=out_specs, check_vma=False)
```
